128 devices in a mesh: seq: 16 (over x_lo, z, core), tp: 8 (over y, x_hi).
Axes of the slice: x: 4 (x_hi: 2, x_lo: 2; x = x_hi * 2 + x_lo), y: 4, z: 4, core: 2. Of those that a mesh axis runs over, the one named last changes fastest.
Arguments:
- prompt_x: bfloat16 [8192, 8192], P('seq'), may hold values from -40 to 40
- w_query: bfloat16 [8192, 4096], P(None, 'tp'), may hold values from -0.0625 to 0.0625
- w_key: bfloat16 [8192, 1024], P(None, 'tp'), may hold values from -0.0625 to 0.0625
- w_value: bfloat16 [8192, 1024], P(None, 'tp'), may hold values from -0.0625 to 0.0625
- decode_x: bfloat16 [4, 256, 8192], P(None, 'seq', 'tp'), may hold values from -40 to 40
- cache_keys: bfloat16 [256, 256, 1024], P('seq', None, 'tp'), may hold values from -6 to 6
- cache_values: bfloat16 [256, 256, 1024], P('seq', None, 'tp'), may hold values from -6 to 6
- cache_len: int32 [256], P('seq'), may hold values from 1 to 256, as said below
- prompt_blocks: int32 [256], P('seq'), may hold values from 1 to 16, as said below
Outputs:
- prefill_out: bfloat16 [8192, 4096], P('seq', 'tp')
- decode_out: bfloat16 [4, 256, 4096], P(None, 'seq', 'tp')
The draws below stay inside these ranges and needn't reach their ends.
Inputs may be any that keep to these rules, and one draw needn't show every extreme that they name: `cache_len`: some row reaches 256. `prompt_blocks`: some row takes all 16 blocks.
All inputs are finite; a program needn't handle non-finite values.
Results may differ from the reference program's by a relative error of at most 0.015.
The reference program's roundings to bfloat16 on the way count: a program that leaves them out, or rounds other values in their place, can miss the bound.
Values may be sent and summed in bfloat16 or wider, within the bound.
A program may use at most 256 MiB of HBM per device.

```python
import math
import jax
import jax.numpy as jnp
from jax import lax

D = 8192
KVH = 8
G = 4
DH = 128
TOK_DEV = 512
CACHE = 256
STEPS = 4
TOKENS = 8192
ROWS = 256
BLOCKS = 16


def draw_prompt_x(key, part):
    key = jax.random.fold_in(key, 11)
    noise_key = jax.random.fold_in(key, 0)
    base_draw = jax.random.normal(noise_key, (TOKENS, D), jnp.float32)
    values = base_draw
    return jnp.clip(values, -40.0, 40.0).astype(jnp.bfloat16)


def draw_decode_x(key, part):
    key = jax.random.fold_in(key, 12)
    noise_key = jax.random.fold_in(key, 0)
    base_draw = jax.random.normal(noise_key, (STEPS, ROWS, D), jnp.float32)
    values = base_draw
    return jnp.clip(values, -40.0, 40.0).astype(jnp.bfloat16)


def draw_cache_len(key, part):
    key = jax.random.fold_in(key, 13)
    value_key, place_key = jax.random.split(key)
    lengths = jax.random.randint(value_key, (ROWS,), 1, CACHE + 1, jnp.int32)
    chosen = jax.random.randint(place_key, (), 0, ROWS, jnp.int32)
    return lengths.at[chosen].set(CACHE)


def draw_prompt_blocks(key, part):
    key = jax.random.fold_in(key, 14)
    value_key, place_key = jax.random.split(key)
    counts = jax.random.randint(value_key, (ROWS,), 1, BLOCKS + 1, jnp.int32)
    chosen = jax.random.randint(place_key, (), 0, ROWS, jnp.int32)
    return counts.at[chosen].set(BLOCKS)


def steps_of(key, dims, cuts, low, high):
    factor_of = 1.0
    for axis_at, shards_of in cuts:
        heights = jax.random.uniform(jax.random.fold_in(jax.random.fold_in(key, 6), axis_at), (shards_of,), jnp.float32, low / len(cuts), high / len(cuts))
        factor_of = factor_of * jnp.repeat(jnp.exp(heights), dims[axis_at] // shards_of).reshape((-1,) + (1,) * (len(dims) - 1 - axis_at))
    return factor_of


def gaussian(rng, dims, scale, reach, cuts=(), kind=jnp.bfloat16):
    values = scale * jax.random.normal(rng, dims, jnp.float32)
    if cuts:
        values = values * steps_of(rng, dims, cuts, -0.22, 0.18)
    return jnp.clip(values, -reach, reach).astype(kind)


def setup_inputs(seed: int = 0) -> dict:
    key_list = jax.random.split(jax.random.key(seed), 10)
    return {
        "prompt_x": draw_prompt_x(jax.random.fold_in(key_list[9], 71), 0),
        "w_query": gaussian(key_list[1], (D, KVH * G * DH), D ** -0.5, 0.0625, ((1, 8),)),
        "w_key": gaussian(key_list[2], (D, KVH * DH), D ** -0.5, 0.0625, ((1, 8),)),
        "w_value": gaussian(key_list[3], (D, KVH * DH), D ** -0.5, 0.0625, ((1, 8),)),
        "decode_x": draw_decode_x(jax.random.fold_in(key_list[9], 71), 0),
        "cache_keys": gaussian(key_list[5], (ROWS, CACHE, KVH * DH), 1.0, 6.0, ((0, 16), (2, 8))),
        "cache_values": gaussian(key_list[6], (ROWS, CACHE, KVH * DH), 1.0, 6.0, ((0, 16), (2, 8))),
        "cache_len": draw_cache_len(jax.random.fold_in(key_list[9], 71), 0),
        "prompt_blocks": draw_prompt_blocks(jax.random.fold_in(key_list[9], 71), 0),
    }


theta_base = 500000.0
neg_big = -1e30


def rotate(values, positions):
    half_size = values.shape[-1] // 2
    index_float = jnp.arange(half_size, dtype=jnp.float32)
    frequency = jnp.exp(index_float * (-2.0 / values.shape[-1] * math.log(theta_base)))
    angle = positions[..., None] * frequency
    cosine = jnp.cos(angle)
    sine_part = jnp.sin(angle)
    first_half = values[..., :half_size]
    second_half = values[..., half_size:]
    return jnp.concatenate([first_half * cosine - second_half * sine_part, second_half * cosine + first_half * sine_part], axis=-1)


def reference(prompt_x, w_query, w_key, w_value, decode_x, cache_keys, cache_values, cache_len, prompt_blocks):
    scale_factor = DH ** -0.5
    positions = jnp.arange(TOKENS, dtype=jnp.int32).astype(jnp.float32)
    queries = rotate(jnp.dot(prompt_x, w_query, preferred_element_type=jnp.float32).reshape(TOKENS, KVH, G, DH), positions[:, None, None]).astype(jnp.bfloat16)
    keys_all = rotate(jnp.dot(prompt_x, w_key, preferred_element_type=jnp.float32).reshape(TOKENS, KVH, DH), positions[:, None]).astype(jnp.bfloat16)
    values_all = jnp.dot(prompt_x, w_value, preferred_element_type=jnp.float32).reshape(TOKENS, KVH, DH).astype(jnp.bfloat16)
    causal = jnp.arange(TOKENS, dtype=jnp.int32)[None, :] <= jnp.arange(TOKENS, dtype=jnp.int32)[:, None]

    def prefill_head(operands):
        head_queries, head_keys, head_values = operands
        scores = jnp.einsum('pgd,sd->pgs', head_queries.astype(jnp.float32), head_keys.astype(jnp.float32)) * scale_factor
        mask_full = causal[:, None, :]
        scores = jnp.where(mask_full, scores, neg_big)
        top_score = scores.max(-1, keepdims=True)
        weights = jnp.where(mask_full, jnp.exp(scores - top_score), 0.0)
        mixed_sum = jnp.einsum('pgs,sd->pgd', weights.astype(jnp.bfloat16).astype(jnp.float32), head_values.astype(jnp.float32))
        return (mixed_sum / weights.sum(-1)[..., None]).astype(jnp.bfloat16)

    prefill_heads = lax.map(prefill_head, (queries.transpose(1, 0, 2, 3), keys_all.transpose(1, 0, 2), values_all.transpose(1, 0, 2)))
    prefill_out = prefill_heads.transpose(1, 0, 2, 3).reshape(TOKENS, KVH * G * DH)

    flat_decode = decode_x.reshape(STEPS * ROWS, D)
    base_pos = prompt_blocks * TOK_DEV + cache_len
    new_pos = (base_pos[None, :] + jnp.arange(STEPS, dtype=jnp.int32)[:, None]).astype(jnp.float32)
    dec_q = rotate(jnp.dot(flat_decode, w_query, preferred_element_type=jnp.float32).reshape(STEPS, ROWS, KVH, G, DH), new_pos[:, :, None, None]).astype(jnp.bfloat16)
    dec_k = rotate(jnp.dot(flat_decode, w_key, preferred_element_type=jnp.float32).reshape(STEPS, ROWS, KVH, DH), new_pos[:, :, None]).astype(jnp.bfloat16)
    dec_v = jnp.dot(flat_decode, w_value, preferred_element_type=jnp.float32).reshape(STEPS, ROWS, KVH, DH).astype(jnp.bfloat16)
    cache_k4 = cache_keys.reshape(ROWS, CACHE, KVH, DH)
    cache_v4 = cache_values.reshape(ROWS, CACHE, KVH, DH)
    prompt_mask = (jnp.arange(TOKENS, dtype=jnp.int32)[None, :] < (prompt_blocks * TOK_DEV)[:, None])[None, :, None, :]
    cache_mask = (jnp.arange(CACHE, dtype=jnp.int32)[None, :] < cache_len[:, None])[None, :, None, :]
    new_mask = (jnp.arange(STEPS, dtype=jnp.int32)[None, :] <= jnp.arange(STEPS, dtype=jnp.int32)[:, None])[:, None, None, :]

    def decode_head(operands):
        head_q, head_k, head_v, prompt_k, prompt_v, head_ck, head_cv = operands
        query_float = head_q.astype(jnp.float32)
        prompt_scores = jnp.einsum('trgd,pd->trgp', query_float, prompt_k.astype(jnp.float32)) * scale_factor
        cache_scores = jnp.einsum('trgd,rld->trgl', query_float, head_ck.astype(jnp.float32)) * scale_factor
        new_scores = jnp.einsum('trgd,urd->trgu', query_float, head_k.astype(jnp.float32)) * scale_factor
        prompt_scores = jnp.where(prompt_mask, prompt_scores, neg_big)
        cache_scores = jnp.where(cache_mask, cache_scores, neg_big)
        new_scores = jnp.where(new_mask, new_scores, neg_big)
        top_score = jnp.maximum(jnp.maximum(prompt_scores.max(-1), cache_scores.max(-1)), new_scores.max(-1))[..., None]
        prompt_w = jnp.where(prompt_mask, jnp.exp(prompt_scores - top_score), 0.0)
        cache_w = jnp.where(cache_mask, jnp.exp(cache_scores - top_score), 0.0)
        new_w = jnp.where(new_mask, jnp.exp(new_scores - top_score), 0.0)
        weight_sum = prompt_w.sum(-1) + cache_w.sum(-1) + new_w.sum(-1)
        mixed_sum = jnp.einsum('trgp,pd->trgd', prompt_w.astype(jnp.bfloat16).astype(jnp.float32), prompt_v.astype(jnp.float32))
        mixed_sum = mixed_sum + jnp.einsum('trgl,rld->trgd', cache_w.astype(jnp.bfloat16).astype(jnp.float32), head_cv.astype(jnp.float32))
        mixed_sum = mixed_sum + jnp.einsum('trgu,urd->trgd', new_w.astype(jnp.bfloat16).astype(jnp.float32), head_v.astype(jnp.float32))
        return (mixed_sum / weight_sum[..., None]).astype(jnp.bfloat16)

    decode_heads = lax.map(decode_head, (dec_q.transpose(2, 0, 1, 3, 4), dec_k.transpose(2, 0, 1, 3), dec_v.transpose(2, 0, 1, 3), keys_all.transpose(1, 0, 2), values_all.transpose(1, 0, 2), cache_k4.transpose(2, 0, 1, 3), cache_v4.transpose(2, 0, 1, 3)))
    decode_out = decode_heads.transpose(1, 2, 0, 3, 4).reshape(STEPS, ROWS, KVH * G * DH)
    return (prefill_out, decode_out)
```

```python
import functools
import math

import jax
import jax.numpy as jnp
import numpy as np
from jax import lax
from jax.experimental import pallas as pl
from jax.experimental.pallas import tpu as pltpu
from jax.sharding import PartitionSpec as P

G = 4
DH = 128
HALF = DH // 2
TOK = 512
KC = 8
KW = 1024
ROWS = 16
STEPS = 4
DQ = STEPS * ROWS * G
TILE = 256
THETA = 500000.0
NEG = -1e30
BIG = 1e30
SC = DH**-0.5 * math.log2(math.e)
BF = jnp.bfloat16
F32 = jnp.float32
MESH = pl.DeviceIdType.MESH


def rope(a, cos, sin):
    return a * cos + pltpu.roll(a, HALF, axis=1) * sin


def dot(a, b):
    return jnp.dot(a, b, preferred_element_type=F32)


def scores(q, k):
    return lax.dot_general(q, k, (((1,), (1,)), ((), ())), preferred_element_type=F32)


def kernel(
    px, wq, wk, wv, dx, ck, cv, clen, pblk, freq, po, do,
    xb, wkv, wqb, kall, vall, xd, ckb, cvb, qs, qd, kd, vd,
    m_s, l_s, acc, accq, acckv, accd, cos_s, sin_s,
    sx, swk, swv, swq, sc, sdx, ss, rk, rv, ssx, rx,
):
    seq = lax.axis_index("seq")
    tp = lax.axis_index("tp")
    core = seq % 2
    chip = seq // 2
    z = chip % 4
    xl = chip // 4

    def at(dxl, dz):
        return ((xl + dxl) % 2) * 4 + (z + dz) % 4

    s_zm = at(0, 3) * 2 + core
    s_zp = at(0, 1) * 2 + core
    s_x = at(1, 0) * 2 + core
    s_zz = at(0, 2) * 2 + core
    s_sib = chip * 2 + (1 - core)
    t_x = (tp // 2) * 2 + (1 - tp % 2)
    t_ym = (tp + 6) % 8
    t_yp = (tp + 2) % 8

    def in_x(c):
        return pltpu.make_async_copy(px.at[:, pl.ds(c * KW, KW)], xb.at[c], sx.at[c])

    def in_wk(c):
        return pltpu.make_async_copy(wk.at[pl.ds(c * KW, KW)], wkv.at[c, :, pl.ds(0, DH)], swk.at[c])

    def in_wv(c):
        return pltpu.make_async_copy(wv.at[pl.ds(c * KW, KW)], wkv.at[c, :, pl.ds(DH, DH)], swv.at[c])

    def in_wq(c):
        return pltpu.make_async_copy(wq.at[pl.ds(c * KW, KW)], wqb.at[c], swq.at[c])

    in_ck = pltpu.make_async_copy(ck, ckb, sc.at[0])
    in_cv = pltpu.make_async_copy(cv, cvb.at[:, :, pl.ds(0, DH)], sc.at[1])
    in_dx = pltpu.make_async_copy(dx, xd.at[tp], sdx)

    barrier = pltpu.get_barrier_semaphore()
    for dev in ((s_zm, tp), (s_zp, tp), (s_x, tp), (s_sib, tp), (seq, t_x), (seq, t_ym), (seq, t_yp)):
        pl.semaphore_signal(barrier, inc=1, device_id=dev, device_id_type=MESH)
    in_dx.start()
    for c in range(KC):
        in_x(c).start()
        in_wk(c).start()
        in_wv(c).start()

    def send_x(p, dev, i):
        return pltpu.make_async_remote_copy(
            src_ref=xd.at[p], dst_ref=xd.at[p], send_sem=ssx.at[i], recv_sem=rx.at[p],
            device_id=(seq, dev), device_id_type=MESH,
        )

    def send_k(b, dev, i):
        return pltpu.make_async_remote_copy(
            src_ref=kall.at[b], dst_ref=kall.at[b], send_sem=ss.at[i], recv_sem=rk.at[b],
            device_id=(dev, tp), device_id_type=MESH,
        )

    def send_v(b, dev, i):
        ref = vall.at[b, :, pl.ds(0, DH)]
        return pltpu.make_async_remote_copy(
            src_ref=ref, dst_ref=ref, send_sem=ss.at[i], recv_sem=rv.at[b],
            device_id=(dev, tp), device_id_type=MESH,
        )

    def got_k(b):
        send_k(b, s_sib, 0).wait_recv()

    def got_v(b):
        send_v(b, s_sib, 0).wait_recv()

    in_dx.wait()
    pl.semaphore_wait(barrier, 7)
    p_x, p_ym, p_yp = t_x, t_ym, t_yp
    x_first = [send_x(tp, t_x, 0), send_x(tp, t_yp, 1), send_x(tp, t_ym, 2)]
    for cp in x_first:
        cp.start()

    lane = lax.broadcasted_iota(jnp.int32, (1, DH), 1)
    sign = jnp.where(lane < HALF, -1.0, 1.0).astype(F32)
    fr = freq[...]
    pos = (lax.broadcasted_iota(jnp.int32, (TOK, DH), 0) + seq * TOK).astype(F32)
    cos_s[...] = jnp.cos(pos * fr)
    sin_s[...] = jnp.sin(pos * fr) * sign
    vall[:, :, pl.ds(DH, DH)] = jnp.ones((16, TOK, DH), BF)
    cvb[:, :, pl.ds(DH, DH)] = jnp.ones((ROWS, 256, DH), BF)
    vd[:, pl.ds(DH, DH)] = jnp.ones((STEPS * ROWS, DH), BF)

    acckv[...] = jnp.zeros_like(acckv)

    def kv_step(c, _):
        in_x(c).wait()
        in_wk(c).wait()
        in_wv(c).wait()

        @pl.when(c >= KC // 2)
        def _():
            in_wq(2 * c - KC).start()
            in_wq(2 * c - KC + 1).start()

        acckv[...] += dot(xb[c], wkv[c])
        return 0

    lax.fori_loop(0, KC, kv_step, 0)
    in_ck.start()
    in_cv.start()
    kall[seq] = rope(acckv[:, :DH], cos_s[...], sin_s[...]).astype(BF)
    vall[seq, :, pl.ds(0, DH)] = acckv[:, DH:].astype(BF)
    for i, dev in enumerate((s_zp, s_zm, s_x, s_sib)):
        send_k(seq, dev, i).start()
    for i, dev in enumerate((s_zm, s_zp, s_x, s_sib)):
        send_v(seq, dev, 4 + i).start()

    got_x = lambda p: send_x(p, t_x, 0).wait_recv()
    got_x(p_x)
    x_second = [send_x(p_x, t_yp, 3), send_x(p_x, t_ym, 4)]
    for cp in x_second:
        cp.start()
    got_x(p_ym)
    x_third = send_x(p_ym, t_yp, 5)
    x_third.start()

    accq[...] = jnp.zeros_like(accq)

    def q_step(c, _):
        in_wq(c).wait()
        accq[...] += dot(xb[c], wqb[c])
        return 0

    lax.fori_loop(0, KC, q_step, 0)
    for g in range(G):
        qs[pl.ds(g * TOK, TOK), :] = rope(
            accq[:, g * DH : (g + 1) * DH], cos_s[...], sin_s[...]
        ).astype(BF)

    p_bp = (t_yp // 2) * 2 + (1 - tp % 2)
    p_bm = (t_ym // 2) * 2 + (1 - tp % 2)
    got_x(p_bp)
    x_fourth = send_x(p_bp, t_ym, 6)
    x_fourth.start()
    got_k(s_zm)
    send_k(s_zm, s_zp, 8).start()
    got_v(s_zp)
    send_v(s_zp, s_zm, 9).start()
    got_k(s_x)
    send_k(s_x, s_zm, 10).start()
    send_k(s_x, s_zp, 11).start()
    got_v(s_x)
    send_v(s_x, s_zm, 12).start()
    send_v(s_x, s_zp, 13).start()
    got_v(s_zm)
    got_k(s_zp)
    order = ((0, 0), (0, 3), (0, 1), (1, 0), (0, 2), (1, 3), (1, 1), (1, 2))

    def to_sib(n, start):
        b = at(*order[n]) * 2 + core
        for cp in (send_k(b, s_sib, 14 + 2 * n), send_v(b, s_sib, 15 + 2 * n)):
            if start:
                cp.start()
            else:
                cp.wait_send()

    for n in (1, 2, 3):
        to_sib(n, True)

    def prefill_chunk(c, first):
        k = kall[pl.ds(2 * c, 2)].reshape(2 * TOK, DH)
        v = vall[pl.ds(2 * c, 2)].reshape(2 * TOK, 2 * DH)
        count = G * TOK // TILE
        if first:
            row = lax.broadcasted_iota(jnp.int32, (TILE, 2 * TOK), 0) + core * TOK
            col = lax.broadcasted_iota(jnp.int32, (TILE, 2 * TOK), 1)
            masks = [col <= row + h * TILE for h in range(TOK // TILE)]
        rows = [pl.ds(u * TILE, TILE) for u in range(count)]
        s_next = scores(qs[rows[0], :], k)
        outs = []
        for u in range(count):
            s = s_next
            if u + 1 < count:
                s_next = scores(qs[rows[u + 1], :], k)
            if first:
                s = jnp.where(masks[u % (TOK // TILE)], s, NEG)
            top = jnp.broadcast_to(jnp.max(s, axis=1, keepdims=True) * SC, (TILE, DH))
            if not first:
                old = m_s[rows[u], :]
                top = jnp.maximum(old, top)
            w = jnp.exp2(s * SC - top[:, :1])
            o = dot(w.astype(BF), v)
            if first:
                outs.append((top, o[:, :DH], o[:, DH:]))
            else:
                fade = jnp.exp2(old - top)
                outs.append((top, acc[rows[u], :] * fade + o[:, :DH], l_s[rows[u], :] * fade + o[:, DH:]))
        for u in range(count):
            m_s[rows[u], :], acc[rows[u], :], l_s[rows[u], :] = outs[u]

    got_k(s_sib)
    got_v(s_sib)
    prefill_chunk(chip, True)

    got_k(s_zz)
    send_k(s_zz, s_x, 30).start()
    got_v(s_zz)
    send_v(s_zz, s_x, 31).start()
    to_sib(4, True)

    for p in (p_yp, p_bm, (tp + 4) % 8, (t_x + 4) % 8):
        got_x(p)
    accd[...] = jnp.zeros_like(accd)

    def d_step(c, _):
        xc = xd[c].reshape(STEPS * ROWS, KW)
        accd[:, : G * DH] += dot(xc, wqb[c])
        accd[:, G * DH :] += dot(xc, wkv[c])
        return 0

    lax.fori_loop(0, KC, d_step, 0)
    rid = lax.broadcasted_iota(jnp.int32, (DQ, DH), 0) % ROWS
    cl = jnp.zeros((DQ, DH), jnp.int32)
    pb = jnp.zeros((DQ, DH), jnp.int32)
    for r in range(ROWS):
        cl = jnp.where(rid == r, clen[r], cl)
        pb = jnp.where(rid == r, pblk[r], pb)
    n_new = STEPS * ROWS
    step_of = lax.broadcasted_iota(jnp.int32, (n_new, DH), 0) // ROWS
    dpos = (pb[:n_new] * TOK + cl[:n_new] + step_of).astype(F32)
    dcos = jnp.cos(dpos * fr)
    dsin = jnp.sin(dpos * fr) * sign
    for g in range(G):
        qd[pl.ds(g * n_new, n_new), :] = rope(accd[:, g * DH : (g + 1) * DH], dcos, dsin).astype(BF)
    kd[...] = rope(accd[:, G * DH : (G + 1) * DH], dcos, dsin).astype(BF)
    vd[:, pl.ds(0, DH)] = accd[:, (G + 1) * DH :].astype(BF)
    in_ck.wait()
    in_cv.wait()

    q = qd[...]
    row = lax.broadcasted_iota(jnp.int32, (DQ, n_new), 0)
    col = lax.broadcasted_iota(jnp.int32, (DQ, n_new), 1)
    keep = (row % ROWS == col % ROWS) & (col // ROWS <= (row % n_new) // ROWS)
    s = jnp.where(keep, scores(q, kd[...]), NEG)
    d_m = jnp.broadcast_to(jnp.max(s, axis=1, keepdims=True) * SC, (DQ, DH))
    w = jnp.exp2(s * SC - d_m[:, :1])
    d_o = dot(w.astype(BF), vd[...])

    at_once = 4
    row = lax.broadcasted_iota(jnp.int32, (DQ, at_once * 256), 0) % ROWS
    col = lax.broadcasted_iota(jnp.int32, (DQ, at_once * 256), 1)
    live = (col % 256) < cl[:, :1]
    for j in range(ROWS // at_once):
        kc = ckb[pl.ds(j * at_once, at_once)].reshape(at_once * 256, DH)
        vc = cvb[pl.ds(j * at_once, at_once)].reshape(at_once * 256, 2 * DH)
        keep = live & (col // 256 + j * at_once == row)
        s = jnp.where(keep, scores(q, kc), NEG)
        top = jnp.maximum(d_m, jnp.max(s, axis=1, keepdims=True) * SC)
        w = jnp.exp2(s * SC - top[:, :1])
        fade = jnp.exp2(d_m - top)
        d_o = d_o * jnp.concatenate([fade, fade], axis=1) + dot(w.astype(BF), vc)
        d_m = top
    dm = pl.ds(G * TOK, DQ)
    m_s[dm, :] = d_m
    acc[dm, :] = d_o[:, :DH]
    l_s[dm, :] = d_o[:, DH:]

    def chunk_step(n, _):
        dxl = jnp.where((n == 3) | (n >= 5), 1, 0)
        dz = jnp.where((n == 1) | (n == 5), 3, jnp.where((n == 2) | (n == 6), 1, jnp.where(n == 3, 0, 2)))
        c = at(dxl, dz)

        @pl.when(n == 3)
        def _():
            for i in (5, 6):
                b = at(*order[i]) * 2 + core
                got_k(b)
                got_v(b)
                to_sib(i, True)

        @pl.when(n == 4)
        def _():
            b = at(*order[7]) * 2 + core
            got_k(b)
            got_v(b)
            to_sib(7, True)

        b = 2 * c + 1 - core
        got_k(b)
        got_v(b)

        @pl.when(c < chip)
        def _():
            prefill_chunk(c, False)

        return 0

    lax.fori_loop(1, 8, chunk_step, 0)

    def dec_step(j, _):
        q = qd[...]
        d_m, d_a, d_l = m_s[dm, :], acc[dm, :], l_s[dm, :]
        for i in range(4):
            c = j * 4 + i
            k = kall[pl.ds(2 * c, 2)].reshape(2 * TOK, DH)
            v = vall[pl.ds(2 * c, 2)].reshape(2 * TOK, 2 * DH)
            s = scores(q, k)
            in0 = pb > 2 * c
            in1 = pb > 2 * c + 1
            top0 = jnp.max(s[:, :TOK], axis=1, keepdims=True) * SC
            top1 = jnp.max(s[:, TOK:], axis=1, keepdims=True) * SC
            top = jnp.maximum(d_m, jnp.maximum(jnp.where(in0, top0, NEG), jnp.where(in1, top1, NEG)))
            w0 = jnp.exp2(s[:, :TOK] * SC - jnp.where(in0, top, BIG)[:, :1])
            w1 = jnp.exp2(s[:, TOK:] * SC - jnp.where(in1, top, BIG)[:, :1])
            fade = jnp.exp2(d_m - top)
            o = dot(w0.astype(BF), v[:TOK]) + dot(w1.astype(BF), v[TOK:])
            d_a = d_a * fade + o[:, :DH]
            d_l = d_l * fade + o[:, DH:]
            d_m = top
        m_s[dm, :] = d_m
        acc[dm, :] = d_a
        l_s[dm, :] = d_l
        return 0

    lax.fori_loop(0, 2, dec_step, 0)
    d_out = (acc[dm, :] / l_s[dm, :]).astype(BF)
    for g in range(G):
        do[:, :, g * DH : (g + 1) * DH] = d_out[g * n_new : (g + 1) * n_new].reshape(STEPS, ROWS, DH)
    for g in range(G):
        r = pl.ds(g * TOK, TOK)
        po[:, g * DH : (g + 1) * DH] = (acc[r, :] / l_s[r, :]).astype(BF)

    for i, dev in enumerate((s_zp, s_zm, s_x, s_sib)):
        send_k(seq, dev, i).wait_send()
    for i, dev in enumerate((s_zm, s_zp, s_x, s_sib)):
        send_v(seq, dev, 4 + i).wait_send()
    send_k(s_zm, s_zp, 8).wait_send()
    send_v(s_zp, s_zm, 9).wait_send()
    send_k(s_x, s_zm, 10).wait_send()
    send_k(s_x, s_zp, 11).wait_send()
    send_v(s_x, s_zm, 12).wait_send()
    send_v(s_x, s_zp, 13).wait_send()
    send_k(s_zz, s_x, 30).wait_send()
    send_v(s_zz, s_x, 31).wait_send()
    for n in range(1, 8):
        to_sib(n, False)
    for cp in x_first + x_second + [x_third, x_fourth]:
        cp.wait_send()


def body(px, wq, wk, wv, dx, ck, cv, clen, pblk):
    index = np.arange(DH) % HALF
    freq = np.exp(index * (-2.0 / DH) * math.log(THETA)).astype(np.float32).reshape(1, DH)
    any_spec = pl.BlockSpec(memory_space=pl.ANY)
    smem = pl.BlockSpec(memory_space=pltpu.SMEM)
    vmem = pl.BlockSpec(memory_space=pltpu.VMEM)
    dma = pltpu.SemaphoreType.DMA
    return pl.pallas_call(
        kernel,
        name="layer",
        out_shape=(
            jax.ShapeDtypeStruct((TOK, G * DH), BF),
            jax.ShapeDtypeStruct((STEPS, ROWS, G * DH), BF),
        ),
        in_specs=[any_spec] * 7 + [smem, smem, vmem],
        out_specs=(vmem, vmem),
        scratch_shapes=[
            pltpu.VMEM((KC, TOK, KW), BF),
            pltpu.VMEM((KC, KW, 2 * DH), BF),
            pltpu.VMEM((KC, KW, G * DH), BF),
            pltpu.VMEM((16, TOK, DH), BF),
            pltpu.VMEM((16, TOK, 2 * DH), BF),
            pltpu.VMEM((8, STEPS, ROWS, KW), BF),
            pltpu.VMEM((ROWS, 256, DH), BF),
            pltpu.VMEM((ROWS, 256, 2 * DH), BF),
            pltpu.VMEM((G * TOK, DH), BF),
            pltpu.VMEM((DQ, DH), BF),
            pltpu.VMEM((STEPS * ROWS, DH), BF),
            pltpu.VMEM((STEPS * ROWS, 2 * DH), BF),
            pltpu.VMEM((G * TOK + DQ, DH), F32),
            pltpu.VMEM((G * TOK + DQ, DH), F32),
            pltpu.VMEM((G * TOK + DQ, DH), F32),
            pltpu.VMEM((TOK, G * DH), F32),
            pltpu.VMEM((TOK, 2 * DH), F32),
            pltpu.VMEM((STEPS * ROWS, (G + 2) * DH), F32),
            pltpu.VMEM((TOK, DH), F32),
            pltpu.VMEM((TOK, DH), F32),
            dma((KC,)), dma((KC,)), dma((KC,)), dma((KC,)), dma((2,)), dma,
            dma((32,)), dma((16,)), dma((16,)), dma((7,)), dma((8,)),
        ],
        compiler_params=pltpu.CompilerParams(
            collective_id=0, has_side_effects=True, vmem_limit_bytes=60 * 2**20
        ),
        cost_estimate=pl.CostEstimate(flops=20 * 10**9, bytes_accessed=26 * 10**6, transcendentals=10**7),
    )(px, wq, wk, wv, dx, ck, cv, clen, pblk, jnp.asarray(freq))


def solution(mesh):
    placed = (
        P("seq", None),
        P(None, "tp"),
        P(None, "tp"),
        P(None, "tp"),
        P(None, "seq", "tp"),
        P("seq", None, "tp"),
        P("seq", None, "tp"),
        P("seq"),
        P("seq"),
    )
    return jax.shard_map(
        body,
        mesh=mesh,
        in_specs=placed,
        out_specs=(P("seq", "tp"), P(None, "seq", "tp")),
        check_vma=False,
    )
```

```python
import functools
import math

import jax
import jax.numpy as jnp
import numpy as np
from jax import lax
from jax.experimental import pallas as pl
from jax.experimental.pallas import tpu as pltpu
from jax.sharding import PartitionSpec as P

G = 4
DH = 128
HALF = DH // 2
TOK = 512
KC = 4
KW = 2048
XP = 8
XW = 1024
ROWS = 16
STEPS = 4
DQ = STEPS * ROWS * G
TILE = 256
THETA = 500000.0
NEG = -1e30
BIG = 1e30
SC = DH**-0.5 * math.log2(math.e)
BF = jnp.bfloat16
F32 = jnp.float32
MESH = pl.DeviceIdType.MESH


def rope(a, cos, sin):
    return a * cos + pltpu.roll(a, HALF, axis=1) * sin


def dot(a, b):
    return jnp.dot(a, b, preferred_element_type=F32)


def scores(q, k):
    return lax.dot_general(q, k, (((1,), (1,)), ((), ())), preferred_element_type=F32)


def kernel(
    px, wq, wk, wv, dx, ck, cv, clen, pblk, freq, po, do,
    xb, wkv, wqb, kall, vall, xd, ckb, cvb, qs, kd, vd,
    m_s, l_s, acc, accq, acckv, accd, cos_s, sin_s, dlim, ob,
    sx, swk, swv, swq, sc, sdx, ss, rk, rv, ssx, rx, sq, rq,
):
    seq = lax.axis_index("seq")
    tp = lax.axis_index("tp")
    core = seq % 2
    chip = seq // 2
    z = chip % 4
    xl = chip // 4

    def at(dxl, dz):
        return ((xl + dxl) % 2) * 4 + (z + dz) % 4

    s_zm = at(0, 3) * 2 + core
    s_zp = at(0, 1) * 2 + core
    s_x = at(1, 0) * 2 + core
    s_zz = at(0, 2) * 2 + core
    s_sib = chip * 2 + (1 - core)
    t_x = (tp // 2) * 2 + (1 - tp % 2)
    t_ym = (tp + 6) % 8
    t_yp = (tp + 2) % 8

    heavy = xl == 1
    mirror = 15 - seq
    far = jnp.where(heavy, chip, 7 - chip)
    give = far - 3
    order = ((0, 0), (0, 3), (0, 1), (1, 0), (0, 2), (1, 3), (1, 1), (1, 2))

    def in_x(c):
        return pltpu.make_async_copy(px.at[:, pl.ds(c * KW, KW)], xb.at[c], sx.at[c])

    def in_wk(c):
        return pltpu.make_async_copy(wk.at[pl.ds(c * KW, KW)], wkv.at[c, :, pl.ds(0, DH)], swk.at[c])

    def in_wv(c):
        return pltpu.make_async_copy(wv.at[pl.ds(c * KW, KW)], wkv.at[c, :, pl.ds(DH, DH)], swv.at[c])

    def in_wq(c):
        return pltpu.make_async_copy(wq.at[pl.ds(c * KW, KW)], wqb.at[c], swq.at[c])

    in_ck = pltpu.make_async_copy(ck, ckb, sc.at[0])
    in_cv = pltpu.make_async_copy(cv, cvb.at[:, :, pl.ds(0, DH)], sc.at[1])
    in_dx = pltpu.make_async_copy(dx, xd.at[tp], sdx)

    barrier = pltpu.get_barrier_semaphore()
    for dev in ((s_zm, tp), (s_zp, tp), (s_x, tp), (s_sib, tp), (seq, t_x), (seq, t_ym), (seq, t_yp), (mirror, tp)):
        pl.semaphore_signal(barrier, inc=1, device_id=dev, device_id_type=MESH)
    in_dx.start()
    for c in range(KC):
        in_x(c).start()
        in_wk(c).start()
        in_wv(c).start()

    def send_x(p, dev, i):
        return pltpu.make_async_remote_copy(
            src_ref=xd.at[p], dst_ref=xd.at[p], send_sem=ssx.at[i], recv_sem=rx.at[p],
            device_id=(seq, dev), device_id_type=MESH,
        )

    def send_k(b, dev, i):
        return pltpu.make_async_remote_copy(
            src_ref=kall.at[b], dst_ref=kall.at[b], send_sem=ss.at[i], recv_sem=rk.at[b],
            device_id=(dev, tp), device_id_type=MESH,
        )

    def send_v(b, dev, i):
        ref = vall.at[b, :, pl.ds(0, DH)]
        return pltpu.make_async_remote_copy(
            src_ref=ref, dst_ref=ref, send_sem=ss.at[i], recv_sem=rv.at[b],
            device_id=(dev, tp), device_id_type=MESH,
        )

    def got_k(b):
        send_k(b, s_sib, 0).wait_recv()

    def got_v(b):
        send_v(b, s_sib, 0).wait_recv()

    in_dx.wait()
    pl.semaphore_wait(barrier, 8)
    p_x, p_ym, p_yp = t_x, t_ym, t_yp
    x_first = [send_x(tp, t_x, 0), send_x(tp, t_yp, 1), send_x(tp, t_ym, 2)]
    for cp in x_first:
        cp.start()

    arrival = [at(dxl, dz) for dxl, dz in order]

    def ranks(top):
        found, out = 0, []
        for c in arrival:
            out.append(jnp.where(c <= top, found, 99))
            found = found + jnp.where(c <= top, 1, 0)
        return out

    own_rank = ranks(chip)
    far_rank = ranks(far)

    lane = lax.broadcasted_iota(jnp.int32, (1, DH), 1)
    sign = jnp.where(lane < HALF, -1.0, 1.0).astype(F32)
    fr = freq[...]
    pos = (lax.broadcasted_iota(jnp.int32, (TOK, DH), 0) + seq * TOK).astype(F32)
    cos_s[...] = jnp.cos(pos * fr)
    sin_s[...] = jnp.sin(pos * fr) * sign
    vall[:, :, pl.ds(DH, DH)] = jnp.ones((16, TOK, DH), BF)
    cvb[:, :, pl.ds(DH, DH)] = jnp.ones((ROWS, 256, DH), BF)
    vd[:, pl.ds(DH, DH)] = jnp.ones((STEPS * ROWS, DH), BF)

    rid = lax.broadcasted_iota(jnp.int32, (DQ, DH), 0) % ROWS
    pb = jnp.zeros((DQ, DH), jnp.int32)
    for r in range(ROWS):
        pb = jnp.where(rid == r, pblk[r], pb)
    dlim[...] = pb * TOK
    qs[pl.ds(13 * TILE, TILE), :] = jnp.zeros((TILE, DH), BF)
    acckv[...] = jnp.zeros_like(acckv)

    def kv_step(c, _):
        in_x(c).wait()
        in_wk(c).wait()
        in_wv(c).wait()

        @pl.when(c >= KC // 2)
        def _():
            in_wq(2 * c - KC).start()
            in_wq(2 * c - KC + 1).start()

        acckv[...] += dot(xb[c], wkv[c])
        return 0

    lax.fori_loop(0, KC, kv_step, 0)
    in_ck.start()
    in_cv.start()
    kall[seq] = rope(acckv[:, :DH], cos_s[...], sin_s[...]).astype(BF)
    vall[seq, :, pl.ds(0, DH)] = acckv[:, DH:].astype(BF)
    for i, dev in enumerate((s_zp, s_zm, s_x, s_sib)):
        send_k(seq, dev, i).start()
    for i, dev in enumerate((s_zm, s_zp, s_x, s_sib)):
        send_v(seq, dev, 4 + i).start()

    got_x = lambda p: send_x(p, t_x, 0).wait_recv()
    got_x(p_x)
    x_second = [send_x(p_x, t_yp, 3), send_x(p_x, t_ym, 4)]
    for cp in x_second:
        cp.start()
    got_x(p_ym)
    x_third = send_x(p_ym, t_yp, 5)
    x_third.start()

    accq[...] = jnp.zeros_like(accq)

    def q_rope(g):
        qs[pl.ds(g * TOK, TOK), :] = rope(
            accq[:, g * DH : (g + 1) * DH], cos_s[...], sin_s[...]
        ).astype(BF)

    def q_step(c, _):
        in_wq(c).wait()
        accq[...] += dot(xb[c], wqb[c])
        return 0

    lax.fori_loop(0, KC, q_step, 0)
    for g in range(G):
        q_rope(g)

    def tile_rows(t):
        return pl.ds(pl.multiple_of(t * TILE, TILE), TILE)

    def send_q(g):
        return pltpu.make_async_remote_copy(
            src_ref=qs.at[tile_rows(8 - give + g)], dst_ref=qs.at[tile_rows(8 + g)],
            send_sem=sq.at[g], recv_sem=rq.at[g], device_id=(mirror, tp), device_id_type=MESH,
        )

    def send_o(g):
        return pltpu.make_async_remote_copy(
            src_ref=ob.at[g], dst_ref=ob.at[g],
            send_sem=sq.at[g], recv_sem=rq.at[g], device_id=(mirror, tp), device_id_type=MESH,
        )

    for g in range(4):

        @pl.when(heavy & (give > g))
        def _(g=g):
            send_q(g).start()

    p_bp = (t_yp // 2) * 2 + (1 - tp % 2)
    p_bm = (t_ym // 2) * 2 + (1 - tp % 2)
    got_k(s_zm)
    send_k(s_zm, s_zp, 8).start()
    got_k(s_x)
    send_k(s_x, s_zm, 10).start()
    send_k(s_x, s_zp, 11).start()
    got_x(p_bp)
    x_fourth = send_x(p_bp, t_ym, 6)
    x_fourth.start()

    def core_block(n):
        return at(*order[n]) * 2 + core

    def to_sib(n, start):
        b = core_block(n)
        for cp in (send_k(b, s_sib, 14 + 2 * n), send_v(b, s_sib, 15 + 2 * n)):
            if start:
                cp.start()
            else:
                cp.wait_send()

    def from_sib(n):
        b = at(*order[n]) * 2 + 1 - core
        got_k(b)
        got_v(b)

    m_s[...] = jnp.full_like(m_s, NEG)
    l_s[...] = jnp.zeros_like(l_s)
    acc[...] = jnp.zeros_like(acc)
    from_sib(0)

    n_new = STEPS * ROWS
    dm = pl.ds(12 * TILE, TILE)

    def decode_project():
        for p in (p_yp, p_bm, (tp + 4) % 8, (t_x + 4) % 8):
            got_x(p)
        accd[...] = jnp.zeros_like(accd)

        def d_step(c, _):
            xc = xd[c].reshape(STEPS * ROWS, XW)
            r = pl.ds(pl.multiple_of(c % 2 * XW, XW), XW)
            accd[:, : G * DH] += dot(xc, wqb[c // 2, r, :])
            accd[:, G * DH :] += dot(xc, wkv[c // 2, r, :])
            return 0

        lax.fori_loop(0, XP, d_step, 0)

    def decode_local():
        cl = jnp.zeros((DQ, DH), jnp.int32)
        for r in range(ROWS):
            cl = jnp.where(rid == r, clen[r], cl)
        step_of = lax.broadcasted_iota(jnp.int32, (n_new, DH), 0) // ROWS
        dpos = (dlim[:n_new, :] + cl[:n_new] + step_of).astype(F32)
        dcos = jnp.cos(dpos * fr)
        dsin = jnp.sin(dpos * fr) * sign
        for g in range(G):
            qs[pl.ds(12 * TILE + g * n_new, n_new), :] = rope(
                accd[:, g * DH : (g + 1) * DH], dcos, dsin
            ).astype(BF)
        kd[...] = rope(accd[:, G * DH : (G + 1) * DH], dcos, dsin).astype(BF)
        vd[:, pl.ds(0, DH)] = accd[:, (G + 1) * DH :].astype(BF)
        in_ck.wait()
        in_cv.wait()

        q = qs[dm, :]
        row = lax.broadcasted_iota(jnp.int32, (DQ, n_new), 0)
        col = lax.broadcasted_iota(jnp.int32, (DQ, n_new), 1)
        keep = (row % ROWS == col % ROWS) & (col // ROWS <= (row % n_new) // ROWS)
        s = jnp.where(keep, scores(q, kd[...]), NEG)
        d_m = jnp.broadcast_to(jnp.max(s, axis=1, keepdims=True) * SC, (DQ, DH))
        w = jnp.exp2(s * SC - d_m[:, :1])
        d_o = dot(w.astype(BF), vd[...])

        at_once = 4
        row = lax.broadcasted_iota(jnp.int32, (DQ, at_once * 256), 0) % ROWS
        col = lax.broadcasted_iota(jnp.int32, (DQ, at_once * 256), 1)
        live = (col % 256) < cl[:, :1]
        for j in range(ROWS // at_once):
            kc = ckb[pl.ds(j * at_once, at_once)].reshape(at_once * 256, DH)
            vc = cvb[pl.ds(j * at_once, at_once)].reshape(at_once * 256, 2 * DH)
            keep = live & (col // 256 + j * at_once == row)
            s = jnp.where(keep, scores(q, kc), NEG)
            top = jnp.maximum(d_m, jnp.max(s, axis=1, keepdims=True) * SC)
            w = jnp.exp2(s * SC - top[:, :1])
            fade = jnp.exp2(d_m - top)
            d_o = d_o * jnp.concatenate([fade, fade], axis=1) + dot(w.astype(BF), vc)
            d_m = top
        m_s[dm, :] = d_m
        acc[dm, :] = d_o[:, :DH]
        l_s[dm, :] = d_o[:, DH:]

    def give_back(g):
        @pl.when(~heavy & (give > g))
        def _():
            r = tile_rows(8 + g)
            ob[g] = (acc[r, :] / l_s[r, :]).astype(BF)
            send_o(g).start()

    tiles = jnp.where(heavy, 8 - give, 8)
    stride = jnp.where(tiles == 7, 8, tiles)
    own_rest = stride * chip
    before = jnp.where(heavy, own_rest, 8 * (jnp.maximum(chip, 1) - 1))
    given = jnp.where(heavy, 0, give * (far + 1))
    row_i = lax.broadcasted_iota(jnp.int32, (TILE, DH), 0)
    col_i = lax.broadcasted_iota(jnp.int32, (TILE, 2 * TOK), 1)

    def wide(a):
        return jnp.concatenate([a] * (2 * TOK // DH), axis=1)

    def item(blk, u):
        i = (blk - 1) * 8 + u
        is_given = (i >= before) & (i < before + given)
        j = jnp.maximum(jnp.where(i >= before + given, i - given, i), 0)
        k = jnp.maximum(i - before, 0)
        late = (give == 4) & (k >= 16)
        g_tile = jnp.where(late, (k // 8 - 2) * 2 + k % 2, k % give)
        g_spot = jnp.where(late, 4 + (k % 8) // 2, k // give)
        t = jnp.where(is_given, 8 + g_tile, j % stride)
        spot = jnp.where(is_given, g_spot, 1 + j // stride)
        none = (i >= own_rest + given) | (~is_given & (j % stride >= tiles))
        first = blk == 0
        last = blk == 5
        t = jnp.where(first, u, jnp.where(last, 12, jnp.where(none, 13, t)))
        t = jnp.where(first & (u >= tiles), 13, t)
        c = chip
        for n in range(1, 8):
            rank = jnp.where(is_given, far_rank[n], own_rank[n])
            c = jnp.where(rank == spot, arrival[n], c)
        c = jnp.where(first | none, chip, c)
        c = jnp.where(last, u, c)
        mine = chip * 1024 + core * TOK + (t % 2) * TILE
        theirs = far * 1024 + (1 - core) * TOK + ((t - give) % 2) * TILE
        start = jnp.where(t < 8, mine, jnp.where(t < 12, theirs, -(2**20))) - c * 1024 + 1
        return t, c, start

    def block(blk):
        items = [item(blk, u) for u in range(8)]

        def item_scores(u):
            t, c, _ = items[u]
            return scores(qs[tile_rows(t), :], kall[pl.ds(2 * c, 2)].reshape(2 * TOK, DH))

        s_next = item_scores(0)
        outs = []
        for u in range(8):
            s = s_next
            if u < 7:
                s_next = item_scores(u + 1)
            t, c, start = items[u]
            lim = jnp.where(t == 12, dlim[...] - c * 1024, row_i + start)
            s = jnp.where(col_i < wide(lim), s, NEG)
            top = jnp.broadcast_to(jnp.max(s, axis=1, keepdims=True) * SC, (TILE, DH))
            w = jnp.exp2(s * SC - wide(top))
            outs.append((top, dot(w.astype(BF), vall[pl.ds(2 * c, 2)].reshape(2 * TOK, 2 * DH))))
        for u in range(8):
            r = tile_rows(items[u][0])
            top, o = outs[u]
            old = m_s[r, :]
            new = jnp.maximum(old, top)
            fade = jnp.exp2(old - new)
            part = jnp.exp2(top - new)
            m_s[r, :] = new
            acc[r, :] = acc[r, :] * fade + o[:, :DH] * part
            l_s[r, :] = l_s[r, :] * fade + o[:, DH:] * part

    def take(n):
        b = core_block(n)
        got_k(b)
        got_v(b)
        to_sib(n, True)

    def from_three():
        for n in (1, 2, 3):
            from_sib(n)

    def phase(ph, _):
        @pl.when(ph == 1)
        def _():
            got_v(s_zp)
            send_v(s_zp, s_zm, 9).start()
            got_v(s_x)
            send_v(s_x, s_zm, 12).start()
            send_v(s_x, s_zp, 13).start()
            got_v(s_zm)
            got_k(s_zp)
            for n in (1, 2, 3):
                to_sib(n, True)

            @pl.when(heavy)
            def _():
                from_three()

        @pl.when(ph == 2)
        def _():
            got_k(s_zz)
            send_k(s_zz, s_x, 30).start()
            got_v(s_zz)
            send_v(s_zz, s_x, 31).start()
            to_sib(4, True)

            @pl.when(~heavy)
            def _():
                from_three()

            for g in range(4):

                @pl.when(~heavy & (give > g))
                def _(g=g):
                    send_q(g).wait_recv()

        @pl.when(ph == 3)
        def _():
            take(5)
            take(6)
            from_sib(4)
            from_sib(5)

        @pl.when(ph == 4)
        def _():
            take(7)
            from_sib(6)

        soon = (chip == 0) | (chip == 2)

        @pl.when(soon & (ph == 4) | ~soon & (ph == 5))
        def _():
            from_sib(7)

        decoding = ph == jnp.where(heavy, 2, 1)

        @pl.when(decoding)
        def _():
            decode_project()
            decode_local()

        @pl.when(~decoding)
        def _():
            block(jnp.where(ph > jnp.where(heavy, 2, 1), ph - 1, ph))

        @pl.when(ph == 4)
        def _():
            give_back(0)
            give_back(1)

            @pl.when(give == 3)
            def _():
                give_back(2)

        @pl.when((ph == 5) & (give == 4))
        def _():
            give_back(2)
            give_back(3)

        return 0

    lax.fori_loop(0, 7, phase, 0)
    d_out = (acc[dm, :] / l_s[dm, :]).astype(BF)
    for g in range(G):
        do[:, :, g * DH : (g + 1) * DH] = d_out[g * n_new : (g + 1) * n_new].reshape(STEPS, ROWS, DH)

    def put(t, o):
        po[(t % 2) * TILE : (t % 2 + 1) * TILE, (t // 2) * DH : (t // 2 + 1) * DH] = o

    for t in range(8):
        own = ~(heavy & (t >= 8 - give))

        @pl.when(own)
        def _(t=t):
            put(t, (acc[tile_rows(t), :] / l_s[tile_rows(t), :]).astype(BF))

    for g in range(4):

        @pl.when(heavy & (give > g))
        def _(g=g):
            send_o(g).wait_recv()

    for t in range(4, 8):

        @pl.when(heavy & (t >= 8 - give))
        def _(t=t):
            put(t, ob[t - 8 + give])

    for g in range(4):

        @pl.when(give > g)
        def _(g=g):
            send_o(g).wait_send()

    for i, dev in enumerate((s_zp, s_zm, s_x, s_sib)):
        send_k(seq, dev, i).wait_send()
    for i, dev in enumerate((s_zm, s_zp, s_x, s_sib)):
        send_v(seq, dev, 4 + i).wait_send()
    send_k(s_zm, s_zp, 8).wait_send()
    send_v(s_zp, s_zm, 9).wait_send()
    send_k(s_x, s_zm, 10).wait_send()
    send_k(s_x, s_zp, 11).wait_send()
    send_v(s_x, s_zm, 12).wait_send()
    send_v(s_x, s_zp, 13).wait_send()
    send_k(s_zz, s_x, 30).wait_send()
    send_v(s_zz, s_x, 31).wait_send()
    for n in range(1, 8):
        to_sib(n, False)
    for cp in x_first + x_second + [x_third, x_fourth]:
        cp.wait_send()


def move(p_in, d_in, p_out, d_out):
    p_out[...] = p_in[...]
    d_out[...] = d_in[...]


def body(px, wq, wk, wv, dx, ck, cv, clen, pblk):
    index = np.arange(DH) % HALF
    freq = np.exp(index * (-2.0 / DH) * math.log(THETA)).astype(np.float32).reshape(1, DH)
    any_spec = pl.BlockSpec(memory_space=pl.ANY)
    smem = pl.BlockSpec(memory_space=pltpu.SMEM)
    vmem = pl.BlockSpec(memory_space=pltpu.VMEM)
    dma = pltpu.SemaphoreType.DMA
    raw = pl.pallas_call(
        kernel,
        name="layer",
        out_shape=(
            jax.ShapeDtypeStruct((TOK, G * DH), BF),
            jax.ShapeDtypeStruct((STEPS, ROWS, G * DH), BF),
        ),
        in_specs=[any_spec] * 7 + [smem, smem, vmem],
        out_specs=(vmem, vmem),
        scratch_shapes=[
            pltpu.VMEM((KC, TOK, KW), BF),
            pltpu.VMEM((KC, KW, 2 * DH), BF),
            pltpu.VMEM((KC, KW, G * DH), BF),
            pltpu.VMEM((16, TOK, DH), BF),
            pltpu.VMEM((16, TOK, 2 * DH), BF),
            pltpu.VMEM((XP, STEPS, ROWS, XW), BF),
            pltpu.VMEM((ROWS, 256, DH), BF),
            pltpu.VMEM((ROWS, 256, 2 * DH), BF),
            pltpu.VMEM((14 * TILE, DH), BF),
            pltpu.VMEM((STEPS * ROWS, DH), BF),
            pltpu.VMEM((STEPS * ROWS, 2 * DH), BF),
            pltpu.VMEM((14 * TILE, DH), F32),
            pltpu.VMEM((14 * TILE, DH), F32),
            pltpu.VMEM((14 * TILE, DH), F32),
            pltpu.VMEM((TOK, G * DH), F32),
            pltpu.VMEM((TOK, 2 * DH), F32),
            pltpu.VMEM((STEPS * ROWS, (G + 2) * DH), F32),
            pltpu.VMEM((TOK, DH), F32),
            pltpu.VMEM((TOK, DH), F32),
            pltpu.VMEM((DQ, DH), jnp.int32),
            pltpu.VMEM((4, TILE, DH), BF),
            dma((KC,)), dma((KC,)), dma((KC,)), dma((KC,)), dma((2,)), dma,
            dma((32,)), dma((16,)), dma((16,)), dma((7,)), dma((8,)), dma((4,)), dma((4,)),
        ],
        compiler_params=pltpu.CompilerParams(
            collective_id=0, has_side_effects=True, vmem_limit_bytes=60 * 2**20
        ),
        cost_estimate=pl.CostEstimate(flops=20 * 10**9, bytes_accessed=26 * 10**6, transcendentals=10**7),
    )(px, wq, wk, wv, dx, ck, cv, clen, pblk, jnp.asarray(freq))
    return pl.pallas_call(
        move,
        name="place",
        out_shape=tuple(jax.ShapeDtypeStruct(o.shape, o.dtype) for o in raw),
        in_specs=[vmem] * 2,
        out_specs=(vmem,) * 2,
    )(*raw)


def solution(mesh):
    placed = (
        P("seq", None),
        P(None, "tp"),
        P(None, "tp"),
        P(None, "tp"),
        P(None, "seq", "tp"),
        P("seq", None, "tp"),
        P("seq", None, "tp"),
        P("seq"),
        P("seq"),
    )
    return jax.shard_map(
        body,
        mesh=mesh,
        in_specs=placed,
        out_specs=(P("seq", "tp"), P(None, "seq", "tp")),
        check_vma=False,
    )
```

```python
import functools
import math

import jax
import jax.numpy as jnp
import numpy as np
from jax import lax
from jax.experimental import pallas as pl
from jax.experimental.pallas import tpu as pltpu
from jax.sharding import PartitionSpec as P

G = 4
DH = 128
HALF = DH // 2
TOK = 512
KC = 4
KW = 2048
XP = 8
XW = 1024
ROWS = 16
STEPS = 4
DQ = STEPS * ROWS * G
TILE = 256
THETA = 500000.0
NEG = -1e30
BIG = 1e30
SC = DH**-0.5 * math.log2(math.e)
BF = jnp.bfloat16
F32 = jnp.float32
MESH = pl.DeviceIdType.MESH


def rope(a, cos, sin):
    return a * cos + pltpu.roll(a, HALF, axis=1) * sin


def dot(a, b):
    return jnp.dot(a, b, preferred_element_type=F32)


def scores(q, k):
    return lax.dot_general(q, k, (((1,), (1,)), ((), ())), preferred_element_type=F32)


def kernel(
    px, wq, wk, wv, dx, ck, cv, clen, pblk, freq, po, do,
    xb, wkv, wqb, kall, vall, xd, ckb, cvb, qs, qd, kd, vd,
    m_s, l_s, acc, accq, acckv, accd, cos_s, sin_s,
    sx, swk, swv, swq, sc, sdx, ss, rk, rv, ssx, rx,
):
    seq = lax.axis_index("seq")
    tp = lax.axis_index("tp")
    core = seq % 2
    chip = seq // 2
    z = chip % 4
    xl = chip // 4

    def at(dxl, dz):
        return ((xl + dxl) % 2) * 4 + (z + dz) % 4

    s_zm = at(0, 3) * 2 + core
    s_zp = at(0, 1) * 2 + core
    s_x = at(1, 0) * 2 + core
    s_zz = at(0, 2) * 2 + core
    s_sib = chip * 2 + (1 - core)
    t_x = (tp // 2) * 2 + (1 - tp % 2)
    t_ym = (tp + 6) % 8
    t_yp = (tp + 2) % 8

    def in_x(c):
        return pltpu.make_async_copy(px.at[:, pl.ds(c * KW, KW)], xb.at[c], sx.at[c])

    def in_wk(c):
        return pltpu.make_async_copy(wk.at[pl.ds(c * KW, KW)], wkv.at[c, :, pl.ds(0, DH)], swk.at[c])

    def in_wv(c):
        return pltpu.make_async_copy(wv.at[pl.ds(c * KW, KW)], wkv.at[c, :, pl.ds(DH, DH)], swv.at[c])

    def in_wq(c):
        return pltpu.make_async_copy(wq.at[pl.ds(c * KW, KW)], wqb.at[c], swq.at[c])

    in_ck = pltpu.make_async_copy(ck, ckb, sc.at[0])
    in_cv = pltpu.make_async_copy(cv, cvb.at[:, :, pl.ds(0, DH)], sc.at[1])
    in_dx = pltpu.make_async_copy(dx, xd.at[tp], sdx)

    barrier = pltpu.get_barrier_semaphore()
    for dev in ((s_zm, tp), (s_zp, tp), (s_x, tp), (s_sib, tp), (seq, t_x), (seq, t_ym), (seq, t_yp)):
        pl.semaphore_signal(barrier, inc=1, device_id=dev, device_id_type=MESH)
    in_dx.start()
    for c in range(KC):
        in_x(c).start()
        in_wk(c).start()
        in_wv(c).start()

    def send_x(p, dev, i):
        return pltpu.make_async_remote_copy(
            src_ref=xd.at[p], dst_ref=xd.at[p], send_sem=ssx.at[i], recv_sem=rx.at[p],
            device_id=(seq, dev), device_id_type=MESH,
        )

    def send_k(b, dev, i):
        return pltpu.make_async_remote_copy(
            src_ref=kall.at[b], dst_ref=kall.at[b], send_sem=ss.at[i], recv_sem=rk.at[b],
            device_id=(dev, tp), device_id_type=MESH,
        )

    def send_v(b, dev, i):
        ref = vall.at[b, :, pl.ds(0, DH)]
        return pltpu.make_async_remote_copy(
            src_ref=ref, dst_ref=ref, send_sem=ss.at[i], recv_sem=rv.at[b],
            device_id=(dev, tp), device_id_type=MESH,
        )

    def got_k(b):
        send_k(b, s_sib, 0).wait_recv()

    def got_v(b):
        send_v(b, s_sib, 0).wait_recv()

    in_dx.wait()
    pl.semaphore_wait(barrier, 7)
    p_x, p_ym, p_yp = t_x, t_ym, t_yp
    x_first = [send_x(tp, t_x, 0), send_x(tp, t_yp, 1), send_x(tp, t_ym, 2)]
    for cp in x_first:
        cp.start()

    lane = lax.broadcasted_iota(jnp.int32, (1, DH), 1)
    sign = jnp.where(lane < HALF, -1.0, 1.0).astype(F32)
    fr = freq[...]
    pos = (lax.broadcasted_iota(jnp.int32, (TOK, DH), 0) + seq * TOK).astype(F32)
    cos_s[...] = jnp.cos(pos * fr)
    sin_s[...] = jnp.sin(pos * fr) * sign
    vall[:, :, pl.ds(DH, DH)] = jnp.ones((16, TOK, DH), BF)
    cvb[:, :, pl.ds(DH, DH)] = jnp.ones((ROWS, 256, DH), BF)
    vd[:, pl.ds(DH, DH)] = jnp.ones((STEPS * ROWS, DH), BF)

    acckv[...] = jnp.zeros_like(acckv)

    def kv_step(c, _):
        in_x(c).wait()
        in_wk(c).wait()
        in_wv(c).wait()

        @pl.when(c >= KC // 2)
        def _():
            in_wq(2 * c - KC).start()
            in_wq(2 * c - KC + 1).start()

        acckv[...] += dot(xb[c], wkv[c])
        return 0

    lax.fori_loop(0, KC, kv_step, 0)
    in_ck.start()
    in_cv.start()
    kall[seq] = rope(acckv[:, :DH], cos_s[...], sin_s[...]).astype(BF)
    vall[seq, :, pl.ds(0, DH)] = acckv[:, DH:].astype(BF)
    for i, dev in enumerate((s_zp, s_zm, s_x, s_sib)):
        send_k(seq, dev, i).start()
    for i, dev in enumerate((s_zm, s_zp, s_x, s_sib)):
        send_v(seq, dev, 4 + i).start()

    got_x = lambda p: send_x(p, t_x, 0).wait_recv()
    got_x(p_x)
    x_second = [send_x(p_x, t_yp, 3), send_x(p_x, t_ym, 4)]
    for cp in x_second:
        cp.start()
    got_x(p_ym)
    x_third = send_x(p_ym, t_yp, 5)
    x_third.start()

    accq[...] = jnp.zeros_like(accq)

    def q_step(c, _):
        in_wq(c).wait()
        accq[...] += dot(xb[c], wqb[c])
        return 0

    lax.fori_loop(0, KC, q_step, 0)
    for g in range(G):
        qs[pl.ds(g * TOK, TOK), :] = rope(
            accq[:, g * DH : (g + 1) * DH], cos_s[...], sin_s[...]
        ).astype(BF)

    p_bp = (t_yp // 2) * 2 + (1 - tp % 2)
    p_bm = (t_ym // 2) * 2 + (1 - tp % 2)
    got_k(s_zm)
    send_k(s_zm, s_zp, 8).start()
    got_v(s_zp)
    send_v(s_zp, s_zm, 9).start()
    got_k(s_x)
    send_k(s_x, s_zm, 10).start()
    send_k(s_x, s_zp, 11).start()
    got_v(s_x)
    send_v(s_x, s_zm, 12).start()
    send_v(s_x, s_zp, 13).start()
    got_v(s_zm)
    got_k(s_zp)
    got_x(p_bp)
    x_fourth = send_x(p_bp, t_ym, 6)
    x_fourth.start()
    order = ((0, 0), (0, 3), (0, 1), (1, 0), (0, 2), (1, 3), (1, 1), (1, 2))

    def to_sib(n, start):
        b = at(*order[n]) * 2 + core
        for cp in (send_k(b, s_sib, 14 + 2 * n), send_v(b, s_sib, 15 + 2 * n)):
            if start:
                cp.start()
            else:
                cp.wait_send()

    for n in (1, 2, 3):
        to_sib(n, True)

    def prefill_chunk(c, first):
        k = kall[pl.ds(2 * c, 2)].reshape(2 * TOK, DH)
        v = vall[pl.ds(2 * c, 2)].reshape(2 * TOK, 2 * DH)
        count = G * TOK // TILE
        if first:
            row = lax.broadcasted_iota(jnp.int32, (TILE, 2 * TOK), 0) + core * TOK
            col = lax.broadcasted_iota(jnp.int32, (TILE, 2 * TOK), 1)
            masks = [col <= row + h * TILE for h in range(TOK // TILE)]
        rows = [pl.ds(u * TILE, TILE) for u in range(count)]
        s_next = scores(qs[rows[0], :], k)
        outs = []
        for u in range(count):
            s = s_next
            if u + 1 < count:
                s_next = scores(qs[rows[u + 1], :], k)
            if first:
                s = jnp.where(masks[u % (TOK // TILE)], s, NEG)
            top = jnp.broadcast_to(jnp.max(s, axis=1, keepdims=True) * SC, (TILE, DH))
            if not first:
                old = m_s[rows[u], :]
                top = jnp.maximum(old, top)
            w = jnp.exp2(s * SC - top[:, :1])
            o = dot(w.astype(BF), v)
            if first:
                outs.append((top, o[:, :DH], o[:, DH:]))
            else:
                fade = jnp.exp2(old - top)
                outs.append((top, acc[rows[u], :] * fade + o[:, :DH], l_s[rows[u], :] * fade + o[:, DH:]))
        for u in range(count):
            m_s[rows[u], :], acc[rows[u], :], l_s[rows[u], :] = outs[u]

    got_k(s_sib)
    got_v(s_sib)
    prefill_chunk(chip, True)

    got_k(s_zz)
    send_k(s_zz, s_x, 30).start()
    got_v(s_zz)
    send_v(s_zz, s_x, 31).start()
    to_sib(4, True)

    for p in (p_yp, p_bm, (tp + 4) % 8, (t_x + 4) % 8):
        got_x(p)
    accd[...] = jnp.zeros_like(accd)

    def d_step(c, _):
        xc = xd[c].reshape(STEPS * ROWS, XW)
        r = pl.ds(pl.multiple_of(c % 2 * XW, XW), XW)
        accd[:, : G * DH] += dot(xc, wqb[c // 2, r, :])
        accd[:, G * DH :] += dot(xc, wkv[c // 2, r, :])
        return 0

    lax.fori_loop(0, XP, d_step, 0)
    rid = lax.broadcasted_iota(jnp.int32, (DQ, DH), 0) % ROWS
    cl = jnp.zeros((DQ, DH), jnp.int32)
    pb = jnp.zeros((DQ, DH), jnp.int32)
    for r in range(ROWS):
        cl = jnp.where(rid == r, clen[r], cl)
        pb = jnp.where(rid == r, pblk[r], pb)
    n_new = STEPS * ROWS
    step_of = lax.broadcasted_iota(jnp.int32, (n_new, DH), 0) // ROWS
    dpos = (pb[:n_new] * TOK + cl[:n_new] + step_of).astype(F32)
    dcos = jnp.cos(dpos * fr)
    dsin = jnp.sin(dpos * fr) * sign
    for g in range(G):
        qd[pl.ds(g * n_new, n_new), :] = rope(accd[:, g * DH : (g + 1) * DH], dcos, dsin).astype(BF)
    kd[...] = rope(accd[:, G * DH : (G + 1) * DH], dcos, dsin).astype(BF)
    vd[:, pl.ds(0, DH)] = accd[:, (G + 1) * DH :].astype(BF)
    in_ck.wait()
    in_cv.wait()

    q = qd[...]
    row = lax.broadcasted_iota(jnp.int32, (DQ, n_new), 0)
    col = lax.broadcasted_iota(jnp.int32, (DQ, n_new), 1)
    keep = (row % ROWS == col % ROWS) & (col // ROWS <= (row % n_new) // ROWS)
    s = jnp.where(keep, scores(q, kd[...]), NEG)
    d_m = jnp.broadcast_to(jnp.max(s, axis=1, keepdims=True) * SC, (DQ, DH))
    w = jnp.exp2(s * SC - d_m[:, :1])
    d_o = dot(w.astype(BF), vd[...])

    at_once = 4
    row = lax.broadcasted_iota(jnp.int32, (DQ, at_once * 256), 0) % ROWS
    col = lax.broadcasted_iota(jnp.int32, (DQ, at_once * 256), 1)
    live = (col % 256) < cl[:, :1]
    for j in range(ROWS // at_once):
        kc = ckb[pl.ds(j * at_once, at_once)].reshape(at_once * 256, DH)
        vc = cvb[pl.ds(j * at_once, at_once)].reshape(at_once * 256, 2 * DH)
        keep = live & (col // 256 + j * at_once == row)
        s = jnp.where(keep, scores(q, kc), NEG)
        top = jnp.maximum(d_m, jnp.max(s, axis=1, keepdims=True) * SC)
        w = jnp.exp2(s * SC - top[:, :1])
        fade = jnp.exp2(d_m - top)
        d_o = d_o * jnp.concatenate([fade, fade], axis=1) + dot(w.astype(BF), vc)
        d_m = top
    dm = pl.ds(G * TOK, DQ)
    m_s[dm, :] = d_m
    acc[dm, :] = d_o[:, :DH]
    l_s[dm, :] = d_o[:, DH:]

    def chunk_step(n, _):
        dxl = jnp.where((n == 3) | (n >= 5), 1, 0)
        dz = jnp.where((n == 1) | (n == 5), 3, jnp.where((n == 2) | (n == 6), 1, jnp.where(n == 3, 0, 2)))
        c = at(dxl, dz)

        @pl.when(n == 3)
        def _():
            for i in (5, 6):
                b = at(*order[i]) * 2 + core
                got_k(b)
                got_v(b)
                to_sib(i, True)

        @pl.when(n == 4)
        def _():
            b = at(*order[7]) * 2 + core
            got_k(b)
            got_v(b)
            to_sib(7, True)

        b = 2 * c + 1 - core
        got_k(b)
        got_v(b)

        @pl.when(c < chip)
        def _():
            prefill_chunk(c, False)

        return 0

    lax.fori_loop(1, 8, chunk_step, 0)

    def dec_step(j, _):
        q = qd[...]
        d_m, d_a, d_l = m_s[dm, :], acc[dm, :], l_s[dm, :]
        for i in range(4):
            c = j * 4 + i
            k = kall[pl.ds(2 * c, 2)].reshape(2 * TOK, DH)
            v = vall[pl.ds(2 * c, 2)].reshape(2 * TOK, 2 * DH)
            s = scores(q, k)
            in0 = pb > 2 * c
            in1 = pb > 2 * c + 1
            top0 = jnp.max(s[:, :TOK], axis=1, keepdims=True) * SC
            top1 = jnp.max(s[:, TOK:], axis=1, keepdims=True) * SC
            top = jnp.maximum(d_m, jnp.maximum(jnp.where(in0, top0, NEG), jnp.where(in1, top1, NEG)))
            w0 = jnp.exp2(s[:, :TOK] * SC - jnp.where(in0, top, BIG)[:, :1])
            w1 = jnp.exp2(s[:, TOK:] * SC - jnp.where(in1, top, BIG)[:, :1])
            fade = jnp.exp2(d_m - top)
            o = dot(w0.astype(BF), v[:TOK]) + dot(w1.astype(BF), v[TOK:])
            d_a = d_a * fade + o[:, :DH]
            d_l = d_l * fade + o[:, DH:]
            d_m = top
        m_s[dm, :] = d_m
        acc[dm, :] = d_a
        l_s[dm, :] = d_l
        return 0

    lax.fori_loop(0, 2, dec_step, 0)
    d_out = (acc[dm, :] / l_s[dm, :]).astype(BF)
    for g in range(G):
        do[:, :, g * DH : (g + 1) * DH] = d_out[g * n_new : (g + 1) * n_new].reshape(STEPS, ROWS, DH)
    for g in range(G):
        r = pl.ds(g * TOK, TOK)
        po[:, g * DH : (g + 1) * DH] = (acc[r, :] / l_s[r, :]).astype(BF)

    for i, dev in enumerate((s_zp, s_zm, s_x, s_sib)):
        send_k(seq, dev, i).wait_send()
    for i, dev in enumerate((s_zm, s_zp, s_x, s_sib)):
        send_v(seq, dev, 4 + i).wait_send()
    send_k(s_zm, s_zp, 8).wait_send()
    send_v(s_zp, s_zm, 9).wait_send()
    send_k(s_x, s_zm, 10).wait_send()
    send_k(s_x, s_zp, 11).wait_send()
    send_v(s_x, s_zm, 12).wait_send()
    send_v(s_x, s_zp, 13).wait_send()
    send_k(s_zz, s_x, 30).wait_send()
    send_v(s_zz, s_x, 31).wait_send()
    for n in range(1, 8):
        to_sib(n, False)
    for cp in x_first + x_second + [x_third, x_fourth]:
        cp.wait_send()


def move(p_in, d_in, p_out, d_out):
    p_out[...] = p_in[...]
    d_out[...] = d_in[...]


def body(px, wq, wk, wv, dx, ck, cv, clen, pblk):
    index = np.arange(DH) % HALF
    freq = np.exp(index * (-2.0 / DH) * math.log(THETA)).astype(np.float32).reshape(1, DH)
    any_spec = pl.BlockSpec(memory_space=pl.ANY)
    smem = pl.BlockSpec(memory_space=pltpu.SMEM)
    vmem = pl.BlockSpec(memory_space=pltpu.VMEM)
    dma = pltpu.SemaphoreType.DMA
    raw = pl.pallas_call(
        kernel,
        name="layer",
        out_shape=(
            jax.ShapeDtypeStruct((TOK, G * DH), BF),
            jax.ShapeDtypeStruct((STEPS, ROWS, G * DH), BF),
        ),
        in_specs=[any_spec] * 7 + [smem, smem, vmem],
        out_specs=(vmem, vmem),
        scratch_shapes=[
            pltpu.VMEM((KC, TOK, KW), BF),
            pltpu.VMEM((KC, KW, 2 * DH), BF),
            pltpu.VMEM((KC, KW, G * DH), BF),
            pltpu.VMEM((16, TOK, DH), BF),
            pltpu.VMEM((16, TOK, 2 * DH), BF),
            pltpu.VMEM((XP, STEPS, ROWS, XW), BF),
            pltpu.VMEM((ROWS, 256, DH), BF),
            pltpu.VMEM((ROWS, 256, 2 * DH), BF),
            pltpu.VMEM((G * TOK, DH), BF),
            pltpu.VMEM((DQ, DH), BF),
            pltpu.VMEM((STEPS * ROWS, DH), BF),
            pltpu.VMEM((STEPS * ROWS, 2 * DH), BF),
            pltpu.VMEM((G * TOK + DQ, DH), F32),
            pltpu.VMEM((G * TOK + DQ, DH), F32),
            pltpu.VMEM((G * TOK + DQ, DH), F32),
            pltpu.VMEM((TOK, G * DH), F32),
            pltpu.VMEM((TOK, 2 * DH), F32),
            pltpu.VMEM((STEPS * ROWS, (G + 2) * DH), F32),
            pltpu.VMEM((TOK, DH), F32),
            pltpu.VMEM((TOK, DH), F32),
            dma((KC,)), dma((KC,)), dma((KC,)), dma((KC,)), dma((2,)), dma,
            dma((32,)), dma((16,)), dma((16,)), dma((7,)), dma((8,)),
        ],
        compiler_params=pltpu.CompilerParams(
            collective_id=0, has_side_effects=True, vmem_limit_bytes=60 * 2**20
        ),
        cost_estimate=pl.CostEstimate(flops=20 * 10**9, bytes_accessed=26 * 10**6, transcendentals=10**7),
    )(px, wq, wk, wv, dx, ck, cv, clen, pblk, jnp.asarray(freq))
    return pl.pallas_call(
        move,
        name="place",
        out_shape=tuple(jax.ShapeDtypeStruct(o.shape, o.dtype) for o in raw),
        in_specs=[vmem] * 2,
        out_specs=(vmem,) * 2,
    )(*raw)


def solution(mesh):
    placed = (
        P("seq", None),
        P(None, "tp"),
        P(None, "tp"),
        P(None, "tp"),
        P(None, "seq", "tp"),
        P("seq", None, "tp"),
        P("seq", None, "tp"),
        P("seq"),
        P("seq"),
    )
    return jax.shard_map(
        body,
        mesh=mesh,
        in_specs=placed,
        out_specs=(P("seq", "tp"), P(None, "seq", "tp")),
        check_vma=False,
    )
```
